256 devices in a mesh: clip: 2 (over y_hi), blk: 16 (over x, y_lo, core), heads: 8 (over z).
Axes of the slice: x: 4, y: 4 (y_hi: 2, y_lo: 2; y = y_hi * 2 + y_lo), z: 8, core: 2. Of those that a mesh axis runs over, the one named last changes fastest.
Arguments:
- queries: bfloat16 [20480, 3072], P(('clip', 'blk', 'heads')), parts along dimension 0, may hold values from -9 to 9
- keys: bfloat16 [20480, 3072], P(('clip', 'blk', 'heads')), parts along dimension 0, may hold values from -9 to 9
- values: bfloat16 [20480, 3072], P(('clip', 'blk', 'heads')), parts along dimension 0, may hold values from -6 to 6
- out_weight: bfloat16 [3072, 5120], P('heads'), may hold values from -0.109375 to 0.109375
Outputs:
- projected: bfloat16 [20480, 5120], P(('clip', 'blk', 'heads')), parts along dimension 0
The draws below stay inside these ranges and needn't reach their ends.
There are 2 independent parts, one for each index of `clip`. The reference program is written for one: setup_inputs(seed, part) draws one part's arguments, and reference() takes and returns one part's arrays. A program takes and returns all parts, laid end to end along the dimension named above; an argument that names none is the same for every part. Nothing has to cross between parts.
All inputs are finite; a program needn't handle non-finite values.
Results may differ from the reference program's by a relative error of at most 0.02.
Values may be sent and summed in bfloat16 or wider, within the bound.
No kernel may reach another device: no remote copies, remote signals or barrier semaphores. Data moves between devices by JAX's collectives and lax.ppermute only.
A program may use at most 128 MiB of HBM per device.

```python
import jax
import jax.numpy as jnp
from jax import lax

HEADS = 24
HDIM = 128
D = 5120
AD = 3072
TOKENS = 10240
N_HEADS = 8


def draw_keys(key, part):
    key = jax.random.fold_in(key, 11)
    result = jnp.clip(1.5 * jax.random.normal(key, (TOKENS, AD), jnp.float32), -6.0, 6.0)
    return result.astype(jnp.bfloat16)


def draw_queries(key, part):
    key = jax.random.fold_in(key, 12)
    result = jnp.clip(1.5 * jax.random.normal(key, (TOKENS, AD), jnp.float32), -6.0, 6.0)
    return result.astype(jnp.bfloat16)


def steps_of(stream_key, shape, shards, least, largest):
    loudness = 1.0
    for dim, shards_of in shards:
        heights = jax.random.uniform(jax.random.fold_in(jax.random.fold_in(stream_key, 6), dim), (shards_of,), jnp.float32, least / len(shards), largest / len(shards))
        loudness = loudness * jnp.repeat(jnp.exp(heights), shape[dim] // shards_of).reshape((-1,) + (1,) * (len(shape) - 1 - dim))
    return loudness


def scatter_about(stream_key, shape, width, bound, pieces=(), kind=jnp.bfloat16):
    level = steps_of(stream_key, shape, pieces, -0.22, 0.18) if pieces else 1.0
    array = jax.random.normal(stream_key, shape, jnp.float32) * width * level
    return jnp.minimum(jnp.maximum(array, -bound), bound).astype(kind)


def setup_inputs(seed: int = 0, part: int = 0) -> dict:
    arg_keys = jax.random.split(jax.random.key(seed), 5)
    part_keys = jax.random.split(jax.random.fold_in(arg_keys[4], part), 5)
    queries = draw_queries(jax.random.fold_in(jax.random.fold_in(arg_keys[4], part), 71), part)
    keys = draw_keys(jax.random.fold_in(jax.random.fold_in(arg_keys[4], part), 71), part)
    values = scatter_about(part_keys[2], (TOKENS, AD), 1.0, 6.0, ((0, 128),))
    out_weight = scatter_about(arg_keys[3], (AD, D), AD ** -0.5, 0.109375, ((0, 8),))
    return dict(queries=queries, keys=keys, values=values, out_weight=out_weight)


def head_attention(head_index, queries, keys, values):
    start = (head_index * HDIM).astype(jnp.int32)
    head_queries = lax.dynamic_slice_in_dim(queries, start, HDIM, 1)
    head_keys = lax.dynamic_slice_in_dim(keys, start, HDIM, 1)
    head_values = lax.dynamic_slice_in_dim(values, start, HDIM, 1)
    scores = jnp.dot(head_queries, head_keys.T, preferred_element_type=jnp.float32) * (HDIM ** -0.5)
    row_max = jnp.max(scores, axis=1, keepdims=True)
    exponent = jnp.exp(scores - row_max)
    totals = jnp.sum(exponent, axis=1)
    weights = exponent.astype(jnp.bfloat16)
    mixed = jnp.dot(weights, head_values, preferred_element_type=jnp.float32) / totals[:, None]
    return mixed.astype(jnp.bfloat16)


def reference(queries, keys, values, out_weight):
    def one_head(head_index):
        return head_attention(head_index, queries, keys, values)

    per_head = lax.map(one_head, jnp.arange(HEADS, dtype=jnp.int32))
    attention = jnp.transpose(per_head, (1, 0, 2)).reshape(TOKENS, AD)
    group_width = AD // N_HEADS
    summed = jnp.zeros((TOKENS, D), jnp.float32)
    for group_index in range(N_HEADS):
        lo_col = group_index * group_width
        partial_value = jnp.dot(attention[:, lo_col:lo_col + group_width], out_weight[lo_col:lo_col + group_width], preferred_element_type=jnp.float32).astype(jnp.bfloat16)
        partial_value = lax.optimization_barrier(partial_value)
        summed = summed + partial_value.astype(jnp.float32)
    return summed.astype(jnp.bfloat16)
```

```python
import functools

import jax
import jax.numpy as jnp
import numpy as np
from jax import lax
from jax.experimental import pallas as pl
from jax.experimental.pallas import tpu as pltpu
from jax.sharding import Mesh
from jax.sharding import PartitionSpec as P

HDIM = 128
SCALE = HDIM**-0.5 * 1.4426950408889634
VMEM = 56 * 1024 * 1024
KEY_TILE = 512
EXTRA = 32


def shift(block, axis, distance):
    n = lax.axis_size(axis)
    if distance % n == 0:
        return block
    return lax.ppermute(block, axis, [(i, (i + distance) % n) for i in range(n)])


def params(*semantics):
    return pltpu.CompilerParams(vmem_limit_bytes=VMEM)


def regroup_kernel(z_ref, q_ref, k_ref, v_ref, out_ref):
    for h in range(out_ref.shape[1]):
        for t, ref in enumerate((q_ref, k_ref, v_ref)):
            out_ref[0, h, t] = ref[:, h * HDIM : (h + 1) * HDIM]


def regroup(z, queries, keys, values, groups):
    rows, full = queries.shape
    width = full // groups
    heads = width // HDIM
    source = pl.BlockSpec((rows, width), lambda i, z: (0, lax.rem(z[0] + i, groups)))
    return pl.pallas_call(
        regroup_kernel,
        grid_spec=pltpu.PrefetchScalarGridSpec(
            num_scalar_prefetch=1,
            grid=(groups,),
            in_specs=[source] * 3,
            out_specs=pl.BlockSpec((1, heads, 3, rows, HDIM), lambda i, z: (i, 0, 0, 0, 0)),
        ),
        out_shape=jax.ShapeDtypeStruct((groups, heads, 3, rows, HDIM), queries.dtype),
        compiler_params=params(),
    )(z, queries, keys, values)


def attend_kernel(q0_ref, q1_ref, near_ref, far_ref, out_ref):
    rows = q0_ref.shape[0]
    tiles = [(r, j) for r in (near_ref, far_ref) for j in range(r.shape[1] // KEY_TILE)]
    which = pl.program_id(0)
    q = jnp.where(which == 0, q0_ref[...], q1_ref[...])

    def scores_of(i):
        ref, j = tiles[i]
        return lax.dot_general(
            q,
            ref[0, j * KEY_TILE : (j + 1) * KEY_TILE],
            (((1,), (1,)), ((), ())),
            preferred_element_type=jnp.float32,
        )

    highest, total = None, None
    scores = scores_of(0)
    for i, (ref, j) in enumerate(tiles):
        later = scores_of(i + 1) if i + 1 < len(tiles) else None
        value = ref[1, j * KEY_TILE : (j + 1) * KEY_TILE]
        value = jnp.concatenate([value, jnp.ones_like(value)], axis=1)
        tile_max = jnp.max(scores, axis=1, keepdims=True)
        new = tile_max if highest is None else jnp.maximum(highest, tile_max)
        weights = jnp.exp2((scores - new) * SCALE).astype(jnp.bfloat16)
        part = jnp.dot(weights, value, preferred_element_type=jnp.float32)
        if highest is None:
            total = part
        else:
            total = total * jnp.exp2((highest - new) * SCALE) + part
        highest, scores = new, later
    sums = total[:, HDIM:]
    out_ref[0, :rows] = (total[:, :HDIM] / sums).astype(jnp.bfloat16)
    logs = highest * SCALE + jnp.log(sums) * 1.4426950408889634
    same = lax.broadcasted_iota(jnp.int32, (HDIM, HDIM), 0) == lax.broadcasted_iota(
        jnp.int32, (HDIM, HDIM), 1
    )
    line = lax.broadcasted_iota(jnp.int32, (8, HDIM), 0)
    packed = jnp.zeros((8, HDIM), jnp.float32)
    for b in range(rows // HDIM):
        row = jnp.sum(
            jnp.where(same, logs[b * HDIM : (b + 1) * HDIM], 0.0), axis=0, keepdims=True
        )
        packed = jnp.where(line == b, row, packed)
    high = packed.astype(jnp.bfloat16).astype(jnp.float32)
    middle = (packed - high).astype(jnp.bfloat16).astype(jnp.float32)
    low = packed - high - middle
    out_ref[0, rows:] = jnp.concatenate(
        [high, middle, low, jnp.zeros_like(low)], axis=0
    ).astype(jnp.bfloat16)


def attend(q0, q1, near, far):
    rows = q0.shape[0]
    keys = near.shape[1] + far.shape[1]
    whole = lambda a: pl.BlockSpec(a.shape, lambda i: (0,) * a.ndim)
    return pl.pallas_call(
        attend_kernel,
        grid=(2,),
        in_specs=[whole(q0), whole(q1), whole(near), whole(far)],
        out_specs=pl.BlockSpec((1, rows + EXTRA, HDIM), lambda i: (i, 0, 0)),
        out_shape=jax.ShapeDtypeStruct((2, rows + EXTRA, HDIM), jnp.bfloat16),
        compiler_params=params(),
        cost_estimate=pl.CostEstimate(
            flops=2 * rows * keys * HDIM * 4 * 2,
            bytes_accessed=keys * HDIM * 4,
            transcendentals=2 * rows * keys,
        ),
    )(q0, q1, near, far)


def merge_kernel(a_ref, b_ref, out_ref):
    rows = out_ref.shape[0]
    same = lax.broadcasted_iota(jnp.int32, (HDIM, HDIM), 0) == lax.broadcasted_iota(
        jnp.int32, (HDIM, HDIM), 1
    )

    def logs(ref):
        extra = ref[rows:].astype(jnp.float32)
        return extra[0:8] + extra[8:16] + extra[16:24]

    difference = logs(b_ref) - logs(a_ref)
    share = 1.0 / (1.0 + jnp.exp2(difference))
    for r in range(rows // HDIM):
        part = slice(r * HDIM, (r + 1) * HDIM)
        column = jnp.sum(jnp.where(same, share[r : r + 1], 0.0), axis=1, keepdims=True)
        a, b = a_ref[part].astype(jnp.float32), b_ref[part].astype(jnp.float32)
        out_ref[part] = (b + (a - b) * column).astype(jnp.bfloat16)


def merge(a, b):
    rows = a.shape[0] - EXTRA
    return pl.pallas_call(
        merge_kernel,
        out_shape=jax.ShapeDtypeStruct((rows, HDIM), jnp.bfloat16),
        compiler_params=params(),
    )(a, b)


def project_kernel(place_ref, *refs):
    *head_refs, near_ref, far_ref, out_ref, total = refs
    half, i = pl.program_id(0), pl.program_id(1)
    attention = jnp.concatenate([r[...] for r in head_refs], axis=1)

    def add(weight_ref):
        part = jnp.dot(attention, weight_ref[...], preferred_element_type=jnp.float32)

        @pl.when(i == 0)
        def _():
            total[...] = part

        @pl.when(i > 0)
        def _():
            total[...] += part

    pl.when(half == 0)(lambda: add(near_ref))
    pl.when(half == 1)(lambda: add(far_ref))

    @pl.when(i == pl.num_programs(1) - 1)
    def _():
        out_ref[...] = total[...].astype(out_ref.dtype)


def project(place, heads, near, far, groups):
    rows = heads[0].shape[0]
    depth, columns = near.shape[0] // groups, near.shape[1]

    def weight(own):
        def index(half, i, place):
            step = jnp.where(half == own, i, 0 if own else groups - 1)
            return (lax.rem(place[0] + step, groups), 0)

        return pl.BlockSpec((depth, columns), index)

    return pl.pallas_call(
        project_kernel,
        grid_spec=pltpu.PrefetchScalarGridSpec(
            num_scalar_prefetch=1,
            grid=(2, groups),
            in_specs=[pl.BlockSpec((rows, HDIM), lambda half, i, place: (0, i)) for _ in heads]
            + [weight(0), weight(1)],
            out_specs=pl.BlockSpec(
                (rows, columns), lambda half, i, place: (0, lax.rem(half + place[1], 2))
            ),
            scratch_shapes=[pltpu.VMEM((rows, columns), jnp.float32)],
        ),
        out_shape=jax.ShapeDtypeStruct((rows, 2 * columns), jnp.bfloat16),
        compiler_params=params(),
    )(place, *heads, near, far)


def per_device(queries, keys, values, out_weight):
    groups, across = lax.axis_size("z"), lax.axis_size("x")
    rows, full = queries.shape
    heads = full // groups // HDIM
    x, z, c = lax.axis_index("x"), lax.axis_index("z"), lax.axis_index("c")
    zc = jnp.stack([z, c]).astype(jnp.int32)

    grouped = regroup(zc[:1], queries, keys, values, groups)
    own = []
    for h in range(heads):
        pieces = [shift(grouped[i, h], "z", i) for i in range(groups)]
        own.append(jnp.concatenate(pieces, axis=1))

    columns = out_weight.shape[1] // across
    half = columns // 2
    mine = lax.dynamic_slice_in_dim(out_weight, x * columns + c * half, half, axis=1)
    mine, own[-1] = lax.optimization_barrier((mine, own[-1]))
    near_weight = lax.all_gather(mine, "z", axis=0, tiled=True)
    far_weight = shift(near_weight, "c", 1)

    collected = []
    for h in range(heads):
        q = own[h][0]
        pair = own[h][1:]
        q_beside = shift(q, "y", 1)
        near = jnp.concatenate([shift(pair, "x", i) for i in range(across)], axis=1)
        far = shift(near, "c", 1)
        partial = attend(q, q_beside, near, far)
        attention = merge(partial[0], shift(partial[1], "y", 1))
        back = [
            shift(attention[i * rows : (i + 1) * rows], "z", -i) for i in range(groups)
        ]
        back = jnp.concatenate(back, axis=1)
        collected.append(
            jnp.concatenate([shift(back, "x", i) for i in range(across)], axis=0)
        )

    projected = project(zc, collected, near_weight, far_weight, groups)
    returned = [
        shift(projected[i * rows : (i + 1) * rows], "x", -i) for i in range(across)
    ]
    twice = jnp.concatenate(returned + returned, axis=1)
    start = lax.rem(across - x, across) * columns
    return lax.dynamic_slice_in_dim(twice, start, across * columns, axis=1)


def solution(mesh):
    clip, blk, z = mesh.devices.shape
    fine = Mesh(np.array(mesh.devices).reshape(clip, blk // 4, 2, 2, z), ("clip", "x", "y", "c", "z"))
    tokens = ("clip", "x", "y", "c", "z")
    return jax.shard_map(
        per_device,
        mesh=fine,
        in_specs=(P(tokens, None), P(tokens, None), P(tokens, None), P("z", None)),
        out_specs=P(tokens, None),
        check_vma=False,
    )
```

```python
import jax
import jax.numpy as jnp
import numpy as np
from jax import lax
from jax.experimental import pallas as pl
from jax.experimental.pallas import tpu as pltpu
from jax.sharding import Mesh
from jax.sharding import PartitionSpec as P

HDIM = 128
LOG2E = 1.4426950408889634
SCALE = HDIM**-0.5 * LOG2E
EXTRA = 32


def shift(block, axis, distance):
    n = lax.axis_size(axis)
    if distance % n == 0:
        return block
    return lax.ppermute(block, axis, [(i, (i + distance) % n) for i in range(n)])


def from_all(block, axis, wait=lambda value: value):
    behind, ahead = shift(block, axis, 1), shift(block, axis, -1)
    middle = block.shape[0] // 2
    onward, backward = wait(behind[:middle]), wait(ahead[middle:])
    return [(block,), (behind,), (ahead,), (shift(onward, axis, 1), shift(backward, axis, -1))]


def after(value, *done):
    return lax.optimization_barrier((value, *done))[0]


def params(mebibytes):
    return pltpu.CompilerParams(vmem_limit_bytes=mebibytes * 1024 * 1024)


def regroup_kernel(q_ref, k_ref, v_ref, queries_ref, pairs_ref):
    groups, heads = queries_ref.shape[:2]
    for g in range(groups):
        for h in range(heads):
            first = (g * heads + h) * HDIM
            queries_ref[g, h] = q_ref[:, first : first + HDIM]
            pairs_ref[g, 2 * h] = k_ref[:, first : first + HDIM]
            pairs_ref[g, 2 * h + 1] = v_ref[:, first : first + HDIM]


def regroup(queries, keys, values, groups):
    rows, full = queries.shape
    heads = full // groups // HDIM
    like = lambda n: jax.ShapeDtypeStruct((groups, n, rows, HDIM), queries.dtype)
    return pl.pallas_call(
        regroup_kernel,
        out_shape=[like(heads), like(2 * heads)],
        compiler_params=params(56),
    )(queries, keys, values)


def diagonal():
    shape = (HDIM, HDIM)
    return lax.broadcasted_iota(jnp.int32, shape, 0) == lax.broadcasted_iota(jnp.int32, shape, 1)


def attend_kernel(q_ref, *refs):
    *pair_refs, out_ref = refs
    groups, _, each, _ = q_ref.shape
    rows = groups * each
    q = q_ref[:, 0].reshape(rows, HDIM)
    tiles, held = [[]], 0
    for ref in pair_refs:
        if held == 2 * groups:
            tiles, held = tiles + [[]], 0
        tiles[-1].append(ref)
        held += ref.shape[0]

    def tile(i, which):
        parts = [ref[:, which].reshape(-1, HDIM) for ref in tiles[i]]
        return jnp.concatenate(parts, axis=0)

    def scores_of(i):
        return lax.dot_general(
            q, tile(i, 0), (((1,), (1,)), ((), ())), preferred_element_type=jnp.float32
        )

    highest, total = None, None
    scores = scores_of(0)
    for i in range(len(tiles)):
        later = scores_of(i + 1) if i + 1 < len(tiles) else None
        value = tile(i, 1)
        value = jnp.concatenate([value, jnp.ones_like(value)], axis=1)
        tile_max = jnp.max(scores, axis=1, keepdims=True)
        new = tile_max if highest is None else jnp.maximum(highest, tile_max)
        weights = jnp.exp2((scores - new) * SCALE).astype(jnp.bfloat16)
        part = jnp.dot(weights, value, preferred_element_type=jnp.float32)
        if highest is None:
            total = part
        else:
            total = total * jnp.exp2((highest - new) * SCALE) + part
        highest, scores = new, later
    sums = total[:, HDIM:]
    out_ref[0, :rows] = (total[:, :HDIM] / sums).astype(jnp.bfloat16)
    logs = highest * SCALE + jnp.log(sums) * LOG2E
    same, line = diagonal(), lax.broadcasted_iota(jnp.int32, (8, HDIM), 0)
    packed = jnp.zeros((8, HDIM), jnp.float32)
    for b in range(rows // HDIM):
        part = logs[b * HDIM : (b + 1) * HDIM]
        row = jnp.sum(jnp.where(same, part, 0.0), axis=0, keepdims=True)
        packed = jnp.where(line == b, row, packed)
    high = packed.astype(jnp.bfloat16).astype(jnp.float32)
    middle = (packed - high).astype(jnp.bfloat16).astype(jnp.float32)
    low = packed - high - middle
    out_ref[0, rows:] = jnp.concatenate(
        [high, middle, low, jnp.zeros_like(low)], axis=0
    ).astype(jnp.bfloat16)


def attend(queries, pairs):
    groups, heads, each, _ = queries.shape
    rows = groups * each
    pair = lambda a: pl.BlockSpec((a.shape[0], 2, each, HDIM), lambda h: (0, h, 0, 0))
    keys = sum(a.shape[0] for a in pairs) * each
    scores = heads * rows * keys
    return pl.pallas_call(
        attend_kernel,
        grid=(heads,),
        in_specs=[pl.BlockSpec((groups, 1, each, HDIM), lambda h: (0, h, 0, 0))]
        + [pair(a) for a in pairs],
        out_specs=pl.BlockSpec((1, rows + EXTRA, HDIM), lambda h: (h, 0, 0)),
        out_shape=jax.ShapeDtypeStruct((heads, rows + EXTRA, HDIM), jnp.bfloat16),
        compiler_params=params(48),
        cost_estimate=pl.CostEstimate(
            flops=scores * HDIM * 4 * 4,
            bytes_accessed=heads * keys * HDIM * 4,
            transcendentals=scores,
        ),
    )(queries, *pairs)


def merge_kernel(a_ref, b_ref, out_ref):
    groups, heads, rows, _ = out_ref.shape
    tokens = groups * rows
    same = diagonal()

    def logs(ref, h):
        extra = ref[h, tokens:].astype(jnp.float32)
        return extra[0:8] + extra[8:16] + extra[16:24]

    for h in range(heads):
        difference = logs(b_ref, h) - logs(a_ref, h)
        share = 1.0 / (1.0 + jnp.exp2(difference))
        columns = [
            jnp.sum(jnp.where(same, share[r : r + 1], 0.0), axis=1, keepdims=True)
            for r in range(tokens // HDIM)
        ]
        column = jnp.concatenate(columns, axis=0)
        for g in range(groups):
            part = slice(g * rows, (g + 1) * rows)
            a, b = a_ref[h, part].astype(jnp.float32), b_ref[h, part].astype(jnp.float32)
            out_ref[g, h] = (b + (a - b) * column[part]).astype(jnp.bfloat16)


def merge(a, b, groups):
    heads, tokens = a.shape[0], a.shape[1] - EXTRA
    shape = (groups, heads, tokens // groups, HDIM)
    return pl.pallas_call(
        merge_kernel,
        out_shape=jax.ShapeDtypeStruct(shape, jnp.bfloat16),
        compiler_params=params(16),
    )(a, b)


def project_kernel(c_ref, in_ref, near_ref, far_ref, out_ref, near, far):
    step = pl.program_id(0)
    groups, heads = in_ref.shape[:2]
    attention = jnp.concatenate(
        [in_ref[g, h] for g in range(groups) for h in range(heads)], axis=1
    )
    for weight_ref, total in ((near_ref, near), (far_ref, far)):
        part = jnp.dot(attention, weight_ref[...], preferred_element_type=jnp.float32)

        @pl.when(step == 0)
        def _(part=part, total=total):
            total[...] = part

        @pl.when(step > 0)
        def _(part=part, total=total):
            total[...] += part

    @pl.when(step == pl.num_programs(0) - 1)
    def _():
        columns = near.shape[1]
        for total, at in ((near, c_ref[0]), (far, 1 - c_ref[0])):
            place = pl.ds(pl.multiple_of(at * columns, HDIM), columns)
            out_ref[:, place] = total[...].astype(out_ref.dtype)


def project(c, attention, near, far):
    groups, heads, rows, _ = attention.shape
    depth, columns = near.shape
    steps = 4
    weight = pl.BlockSpec((depth // steps, columns), lambda i, c: (i, 0))
    return pl.pallas_call(
        project_kernel,
        grid_spec=pltpu.PrefetchScalarGridSpec(
            num_scalar_prefetch=1,
            grid=(steps,),
            in_specs=[
                pl.BlockSpec((groups // steps, heads, rows, HDIM), lambda i, c: (i, 0, 0, 0)),
                weight,
                weight,
            ],
            out_specs=pl.BlockSpec((rows, 2 * columns), lambda i, c: (0, 0)),
            scratch_shapes=[pltpu.VMEM((rows, columns), jnp.float32)] * 2,
        ),
        out_shape=jax.ShapeDtypeStruct((rows, 2 * columns), jnp.bfloat16),
        compiler_params=params(16),
        cost_estimate=pl.CostEstimate(
            flops=4 * rows * depth * columns, bytes_accessed=depth * columns * 4, transcendentals=0
        ),
    )(c, attention, near, far)


def place_kernel(x_ref, *refs):
    *in_refs, out_ref = refs
    columns = in_refs[0].shape[1]
    for i, ref in enumerate(in_refs):
        at = lax.rem(x_ref[0] + i, len(in_refs)) * columns
        out_ref[:, pl.ds(pl.multiple_of(at, HDIM), columns)] = ref[...]


def place(x, pieces):
    rows, columns = pieces[0].shape
    whole = pl.BlockSpec((rows, columns), lambda i, x: (0, 0))
    return pl.pallas_call(
        place_kernel,
        grid_spec=pltpu.PrefetchScalarGridSpec(
            num_scalar_prefetch=1,
            grid=(1,),
            in_specs=[whole] * len(pieces),
            out_specs=pl.BlockSpec((rows, len(pieces) * columns), lambda i, x: (0, 0)),
        ),
        out_shape=jax.ShapeDtypeStruct((rows, len(pieces) * columns), pieces[0].dtype),
        compiler_params=params(16),
    )(x, *pieces)


def per_device(queries, keys, values, out_weight):
    groups, across = lax.axis_size("z"), lax.axis_size("x")
    x, c = lax.axis_index("x"), lax.axis_index("c")

    grouped, grouped_pairs = regroup(queries, keys, values, groups)
    pairs = lax.all_to_all(grouped_pairs, "z", 0, 0, tiled=True)
    moved = from_all(pairs, "x")
    q = lax.all_to_all(after(grouped, pairs), "z", 0, 0, tiled=True)
    q_beside = shift(after(q, *moved[1], *moved[2]), "y", 1)

    columns = out_weight.shape[1] // across
    half = columns // 2
    mine = lax.dynamic_slice_in_dim(after(out_weight, pairs), x * columns + c * half, half, axis=1)
    weight = lax.all_gather(mine, "z", axis=0, tiled=True)

    all_pairs = [part for piece in moved for part in (*piece, *(shift(p, "c", 1) for p in piece))]
    partial_beside = attend(q_beside, all_pairs)
    partial = attend(after(q, partial_beside), all_pairs)
    attention = merge(partial, shift(partial_beside, "y", 1), groups)

    back = lax.all_to_all(attention, "z", 0, 0, tiled=True)
    weight_beside = shift(after(weight, attention), "c", 1)
    place_c = c.astype(jnp.int32)[None]
    last = project(place_c, back, weight, weight_beside)
    returned = [last]
    there = from_all(back, "x", lambda value: after(value, last))
    for (piece, *rest), distance in zip(there[1:], (1, -1, 2)):
        piece = jnp.concatenate([piece, *rest], axis=0) if rest else piece
        last = project(place_c, after(piece, last), weight, weight_beside)
        returned.append(shift(last, "x", -distance))
    own, ahead, behind, over = returned
    return place(x.astype(jnp.int32)[None], [own, ahead, over, behind])


def solution(mesh):
    clip, blk, z = mesh.devices.shape
    devices = np.array(mesh.devices).reshape(clip, blk // 4, 2, 2, z)
    tokens = ("clip", "x", "y", "c", "z")
    return jax.shard_map(
        per_device,
        mesh=Mesh(devices, tokens),
        in_specs=(P(tokens, None), P(tokens, None), P(tokens, None), P("z", None)),
        out_specs=P(tokens, None),
        check_vma=False,
    )
```

```python
import functools

import jax
import jax.numpy as jnp
import numpy as np
from jax import lax
from jax.experimental import pallas as pl
from jax.experimental.pallas import tpu as pltpu
from jax.sharding import Mesh
from jax.sharding import PartitionSpec as P

HDIM = 128
LOG2E = 1.4426950408889634
SCALE = HDIM**-0.5 * LOG2E
EXTRA = 32


def shift(block, axis, distance):
    n = lax.axis_size(axis)
    if distance % n == 0:
        return block
    return lax.ppermute(block, axis, [(i, (i + distance) % n) for i in range(n)])


def ring(block, axis):
    middle = block.shape[0] // 2
    low, high = block[:middle], block[middle:]
    behind_low, ahead_high = shift(low, axis, 1), shift(high, axis, -1)
    behind_high, ahead_low = shift(high, axis, 1), shift(low, axis, -1)
    across = [shift(behind_low, axis, 1), shift(ahead_high, axis, -1)]
    return [block], [behind_low, behind_high], [ahead_low, ahead_high], across


def two_steps(block, axis):
    behind, ahead = shift(block, axis, 1), shift(block, axis, -1)
    middle = block.shape[0] // 2
    return [block], [behind], [ahead], [shift(behind[:middle], axis, 1), shift(ahead[middle:], axis, -1)]


def after(value, *done):
    return lax.optimization_barrier((value, *done))[0]


def params(mebibytes):
    return pltpu.CompilerParams(vmem_limit_bytes=mebibytes * 1024 * 1024)


def regroup_kernel(at_ref, q_ref, k_ref, v_ref, weight_ref, queries_ref, pairs_ref, columns_ref):
    groups, heads = queries_ref.shape[:2]
    for g in range(groups):
        for h in range(heads):
            part = slice((g * heads + h) * HDIM, (g * heads + h + 1) * HDIM)
            queries_ref[g, h] = q_ref[:, part]
            pairs_ref[g, 2 * h] = k_ref[:, part]
            pairs_ref[g, 2 * h + 1] = v_ref[:, part]
    columns_ref[...] = weight_ref[...]


def regroup(at, queries, keys, values, out_weight, columns, groups):
    rows, full = queries.shape
    heads = full // groups // HDIM
    block = pl.BlockSpec((out_weight.shape[0], columns), lambda i, at: (0, at[0]))
    whole = lambda a: pl.BlockSpec(a.shape, lambda i, at: (0,) * len(a.shape))
    shapes = [
        jax.ShapeDtypeStruct((groups, heads, rows, HDIM), queries.dtype),
        jax.ShapeDtypeStruct((groups, 2 * heads, rows, HDIM), queries.dtype),
        jax.ShapeDtypeStruct((out_weight.shape[0], columns), out_weight.dtype),
    ]
    return pl.pallas_call(
        regroup_kernel,
        grid_spec=pltpu.PrefetchScalarGridSpec(
            num_scalar_prefetch=1,
            grid=(1,),
            in_specs=[whole(queries)] * 3 + [block],
            out_specs=[whole(a) for a in shapes],
        ),
        out_shape=shapes,
        compiler_params=params(56),
    )(at, queries, keys, values, out_weight)


def diagonal():
    shape = (HDIM, HDIM)
    return lax.broadcasted_iota(jnp.int32, shape, 0) == lax.broadcasted_iota(jnp.int32, shape, 1)


def attend_kernel(q_ref, *refs):
    *pair_refs, out_ref = refs
    groups, _, each, _ = q_ref.shape
    rows = groups * each
    q = q_ref[:, 0].reshape(rows, HDIM)
    tiles, held = [[]], 0
    for ref in pair_refs:
        if held == 2 * groups:
            tiles, held = tiles + [[]], 0
        tiles[-1].append(ref)
        held += ref.shape[0]

    def tile(i, which):
        parts = [ref[:, which].reshape(-1, HDIM) for ref in tiles[i]]
        return jnp.concatenate(parts, axis=0)

    def scores_of(i):
        return lax.dot_general(
            q, tile(i, 0), (((1,), (1,)), ((), ())), preferred_element_type=jnp.float32
        )

    highest, total = None, None
    scores = scores_of(0)
    for i in range(len(tiles)):
        later = scores_of(i + 1) if i + 1 < len(tiles) else None
        value = tile(i, 1)
        value = jnp.concatenate([value, jnp.ones_like(value)], axis=1)
        tile_max = jnp.max(scores, axis=1, keepdims=True)
        new = tile_max if highest is None else jnp.maximum(highest, tile_max)
        weights = jnp.exp2((scores - new) * SCALE).astype(jnp.bfloat16)
        part = jnp.dot(weights, value, preferred_element_type=jnp.float32)
        if highest is None:
            total = part
        else:
            total = total * jnp.exp2((highest - new) * SCALE) + part
        highest, scores = new, later
    sums = total[:, HDIM:]
    out_ref[0, :rows] = (total[:, :HDIM] / sums).astype(jnp.bfloat16)
    logs = highest * SCALE + jnp.log(sums) * LOG2E
    same, line = diagonal(), lax.broadcasted_iota(jnp.int32, (8, HDIM), 0)
    packed = jnp.zeros((8, HDIM), jnp.float32)
    for b in range(rows // HDIM):
        part = logs[b * HDIM : (b + 1) * HDIM]
        row = jnp.sum(jnp.where(same, part, 0.0), axis=0, keepdims=True)
        packed = jnp.where(line == b, row, packed)
    high = packed.astype(jnp.bfloat16).astype(jnp.float32)
    middle = (packed - high).astype(jnp.bfloat16).astype(jnp.float32)
    low = packed - high - middle
    out_ref[0, rows:] = jnp.concatenate(
        [high, middle, low, jnp.zeros_like(low)], axis=0
    ).astype(jnp.bfloat16)


def attend(queries, pairs):
    groups, heads, each, _ = queries.shape
    rows = groups * each
    pair = lambda a: pl.BlockSpec((a.shape[0], 2, each, HDIM), lambda h: (0, h, 0, 0))
    keys = sum(a.shape[0] for a in pairs) * each
    scores = heads * rows * keys
    return pl.pallas_call(
        attend_kernel,
        grid=(heads,),
        in_specs=[pl.BlockSpec((groups, 1, each, HDIM), lambda h: (0, h, 0, 0))]
        + [pair(a) for a in pairs],
        out_specs=pl.BlockSpec((1, rows + EXTRA, HDIM), lambda h: (h, 0, 0)),
        out_shape=jax.ShapeDtypeStruct((heads, rows + EXTRA, HDIM), jnp.bfloat16),
        compiler_params=params(48),
        cost_estimate=pl.CostEstimate(
            flops=scores * HDIM * 4 * 4,
            bytes_accessed=heads * keys * HDIM * 4,
            transcendentals=scores,
        ),
    )(queries, *pairs)


def merge_kernel(a_ref, b_ref, out_ref):
    groups, heads, rows, _ = out_ref.shape
    tokens = groups * rows
    same = diagonal()

    def logs(ref, h):
        extra = ref[h, tokens:].astype(jnp.float32)
        return extra[0:8] + extra[8:16] + extra[16:24]

    for h in range(heads):
        difference = logs(b_ref, h) - logs(a_ref, h)
        share = 1.0 / (1.0 + jnp.exp2(difference))
        columns = [
            jnp.sum(jnp.where(same, share[r : r + 1], 0.0), axis=1, keepdims=True)
            for r in range(tokens // HDIM)
        ]
        column = jnp.concatenate(columns, axis=0)
        for g in range(groups):
            part = slice(g * rows, (g + 1) * rows)
            a, b = a_ref[h, part].astype(jnp.float32), b_ref[h, part].astype(jnp.float32)
            out_ref[g, h] = (b + (a - b) * column[part]).astype(jnp.bfloat16)


def merge(a, b, groups):
    heads, tokens = a.shape[0], a.shape[1] - EXTRA
    shape = (groups, heads, tokens // groups, HDIM)
    return pl.pallas_call(
        merge_kernel,
        out_shape=jax.ShapeDtypeStruct(shape, jnp.bfloat16),
        compiler_params=params(16),
    )(a, b)


def project_kernel(c_ref, *refs, pieces):
    low_refs, high_refs = refs[:pieces], refs[pieces : 2 * pieces]
    near_ref, far_ref, *out_refs, near, far = refs[2 * pieces :]
    step, steps = pl.program_id(0), pl.num_programs(0)
    groups, heads, rows, _ = low_refs[0].shape
    flat = lambda ref: jnp.concatenate([ref[g, h] for g in range(groups) for h in range(heads)], axis=1)
    attention = jnp.concatenate(
        [jnp.where(step < steps // 2, flat(low), flat(high)) for low, high in zip(low_refs, high_refs)],
        axis=0,
    )
    for weight_ref, total in ((near_ref, near), (far_ref, far)):
        part = jnp.dot(attention, weight_ref[...], preferred_element_type=jnp.float32)

        @pl.when(step == 0)
        def _(part=part, total=total):
            total[...] = part

        @pl.when(step > 0)
        def _(part=part, total=total):
            total[...] += part

    @pl.when(step == steps - 1)
    def _():
        columns = near.shape[1]
        for total, at in ((near, c_ref[0]), (far, 1 - c_ref[0])):
            place = pl.ds(pl.multiple_of(at * columns, HDIM), columns)
            for p, out_ref in enumerate(out_refs):
                out_ref[:, place] = total[p * rows : (p + 1) * rows].astype(out_ref.dtype)


def project(c, pieces, near, far):
    depth, columns = near.shape
    steps = 4
    lows, highs = [piece[0] for piece in pieces], [piece[-1] for piece in pieces]
    _, heads, rows, _ = lows[0].shape
    groups = depth // heads // HDIM // steps
    first = 0 if len(pieces[0]) == 2 else steps // 2
    part = (groups, heads, rows, HDIM)
    low = pl.BlockSpec(part, lambda i, c: (jnp.minimum(i, steps // 2 - 1), 0, 0, 0))
    high = pl.BlockSpec(part, lambda i, c: (jnp.maximum(i - steps // 2, 0) + first, 0, 0, 0))
    weight = pl.BlockSpec((depth // steps, columns), lambda i, c: (i, 0))
    out = jax.ShapeDtypeStruct((rows, 2 * columns), jnp.bfloat16)
    return pl.pallas_call(
        functools.partial(project_kernel, pieces=len(pieces)),
        grid_spec=pltpu.PrefetchScalarGridSpec(
            num_scalar_prefetch=1,
            grid=(steps,),
            in_specs=[low] * len(pieces) + [high] * len(pieces) + [weight, weight],
            out_specs=[pl.BlockSpec(out.shape, lambda i, c: (0, 0))] * len(pieces),
            scratch_shapes=[pltpu.VMEM((len(pieces) * rows, columns), jnp.float32)] * 2,
        ),
        out_shape=[out] * len(pieces),
        compiler_params=params(16),
    )(c, *lows, *highs, near, far)


def place_kernel(x_ref, *refs):
    *in_refs, out_ref = refs
    columns = in_refs[0].shape[1]
    for i, ref in enumerate(in_refs):
        at = lax.rem(x_ref[0] + i, len(in_refs)) * columns
        out_ref[:, pl.ds(pl.multiple_of(at, HDIM), columns)] = ref[...]


def place(x, pieces):
    rows, columns = pieces[0].shape
    whole = pl.BlockSpec((rows, columns), lambda i, x: (0, 0))
    return pl.pallas_call(
        place_kernel,
        grid_spec=pltpu.PrefetchScalarGridSpec(
            num_scalar_prefetch=1,
            grid=(1,),
            in_specs=[whole] * len(pieces),
            out_specs=pl.BlockSpec((rows, len(pieces) * columns), lambda i, x: (0, 0)),
        ),
        out_shape=jax.ShapeDtypeStruct((rows, len(pieces) * columns), pieces[0].dtype),
        compiler_params=params(16),
    )(x, *pieces)


def per_device(queries, keys, values, out_weight):
    groups, across = lax.axis_size("z"), lax.axis_size("x")
    x, c = (lax.axis_index(axis).astype(jnp.int32)[None] for axis in ("x", "c"))
    half = out_weight.shape[1] // across // 2

    grouped, pairs, columns = regroup(2 * x + c, queries, keys, values, out_weight, half, groups)
    pairs = lax.all_to_all(pairs, "z", 0, 0, tiled=True)
    weight = lax.all_gather(after(columns, pairs), "z", axis=0, tiled=True)
    own, behind, ahead, over = two_steps(pairs, "x")
    q = lax.all_to_all(after(grouped, pairs), "z", 0, 0, tiled=True)
    q_beside = shift(after(q, *behind, *ahead), "y", 1)

    every = [part for p in (own, behind, ahead, over) for part in (*p, *(shift(b, "c", 1) for b in p))]
    partial_beside = attend(q_beside, every)
    partial = attend(after(q, partial_beside), every)
    attention = merge(partial, shift(partial_beside, "y", 1), groups)
    weight_beside = shift(after(weight, attention), "c", 1)

    back = lax.all_to_all(attention, "z", 0, 0, tiled=True)
    own, behind, ahead, over = ring(back, "x")
    returned, done = [], ()
    for pieces, distances in (((own,), (0,)), ((behind, ahead), (1, -1)), ((over,), (2,))):
        pieces = [[after(part, *done) for part in piece] for piece in pieces]
        done = project(c, pieces, weight, weight_beside)
        returned += [shift(block, "x", -distance) for block, distance in zip(done, distances)]
    own, ahead, behind, over = returned
    return place(x, [own, ahead, over, behind])


def solution(mesh):
    clip, blk, z = mesh.devices.shape
    devices = np.array(mesh.devices).reshape(clip, blk // 4, 2, 2, z)
    tokens = ("clip", "x", "y", "c", "z")
    return jax.shard_map(
        per_device,
        mesh=Mesh(devices, tokens),
        in_specs=(P(tokens, None), P(tokens, None), P(tokens, None), P("z", None)),
        out_specs=P(tokens, None),
        check_vma=False,
    )
```

```python
import functools

import jax
import jax.numpy as jnp
import numpy as np
from jax import lax
from jax.experimental import pallas as pl
from jax.experimental.pallas import tpu as pltpu
from jax.sharding import Mesh
from jax.sharding import PartitionSpec as P

HDIM = 128
LOG2E = 1.4426950408889634
SCALE = HDIM**-0.5 * LOG2E
EXTRA = 32


def shift(block, axis, distance):
    n = lax.axis_size(axis)
    if distance % n == 0:
        return block
    return lax.ppermute(block, axis, [(i, (i + distance) % n) for i in range(n)])


def ring(block, axis):
    middle = block.shape[0] // 2
    low, high = block[:middle], block[middle:]
    behind_low, ahead_high = shift(low, axis, 1), shift(high, axis, -1)
    behind_high, ahead_low = shift(high, axis, 1), shift(low, axis, -1)
    across = [shift(behind_low, axis, 1), shift(ahead_high, axis, -1)]
    return [block], [behind_low, behind_high], [ahead_low, ahead_high], across


def two_steps(block, axis):
    behind, ahead = shift(block, axis, 1), shift(block, axis, -1)
    middle = block.shape[0] // 2
    return [block], [behind], [ahead], [shift(behind[:middle], axis, 1), shift(ahead[middle:], axis, -1)]


def after(value, *done):
    return lax.optimization_barrier((value, *done))[0]


def params(mebibytes):
    return pltpu.CompilerParams(vmem_limit_bytes=mebibytes * 1024 * 1024)


def regroup_kernel(at_ref, q_ref, k_ref, v_ref, weight_ref, queries_ref, pairs_ref, columns_ref):
    groups, heads = queries_ref.shape[:2]
    for g in range(groups):
        for h in range(heads):
            part = slice((g * heads + h) * HDIM, (g * heads + h + 1) * HDIM)
            queries_ref[g, h] = q_ref[:, part]
            pairs_ref[g, 2 * h] = k_ref[:, part]
            pairs_ref[g, 2 * h + 1] = v_ref[:, part]
    columns_ref[...] = weight_ref[...]


def regroup(at, queries, keys, values, out_weight, columns, groups):
    rows, full = queries.shape
    heads = full // groups // HDIM
    block = pl.BlockSpec((out_weight.shape[0], columns), lambda i, at: (0, at[0]))
    whole = lambda a: pl.BlockSpec(a.shape, lambda i, at: (0,) * len(a.shape))
    shapes = [
        jax.ShapeDtypeStruct((groups, heads, rows, HDIM), queries.dtype),
        jax.ShapeDtypeStruct((groups, 2 * heads, rows, HDIM), queries.dtype),
        jax.ShapeDtypeStruct((out_weight.shape[0], columns), out_weight.dtype),
    ]
    return pl.pallas_call(
        regroup_kernel,
        grid_spec=pltpu.PrefetchScalarGridSpec(
            num_scalar_prefetch=1,
            grid=(1,),
            in_specs=[whole(queries)] * 3 + [block],
            out_specs=[whole(a) for a in shapes],
        ),
        out_shape=shapes,
        compiler_params=params(56),
    )(at, queries, keys, values, out_weight)


def diagonal():
    shape = (HDIM, HDIM)
    return lax.broadcasted_iota(jnp.int32, shape, 0) == lax.broadcasted_iota(jnp.int32, shape, 1)


def attend_kernel(q_ref, *refs):
    *pair_refs, out_ref = refs
    groups, _, each, _ = q_ref.shape
    rows = groups * each
    q = q_ref[:, 0].reshape(rows, HDIM)
    tiles, held = [[]], 0
    for ref in pair_refs:
        if held == 2 * groups:
            tiles, held = tiles + [[]], 0
        tiles[-1].append(ref)
        held += ref.shape[0]

    def tile(i, which):
        parts = [ref[:, which].reshape(-1, HDIM) for ref in tiles[i]]
        return jnp.concatenate(parts, axis=0)

    def scores_of(i):
        return lax.dot_general(
            q, tile(i, 0), (((1,), (1,)), ((), ())), preferred_element_type=jnp.float32
        )

    highest, total = None, None
    scores = scores_of(0)
    for i in range(len(tiles)):
        later = scores_of(i + 1) if i + 1 < len(tiles) else None
        value = tile(i, 1)
        value = jnp.concatenate([value, jnp.ones_like(value)], axis=1)
        tile_max = jnp.max(scores, axis=1, keepdims=True)
        new = tile_max if highest is None else jnp.maximum(highest, tile_max)
        weights = jnp.exp2((scores - new) * SCALE).astype(jnp.bfloat16)
        part = jnp.dot(weights, value, preferred_element_type=jnp.float32)
        if highest is None:
            total = part
        else:
            total = total * jnp.exp2((highest - new) * SCALE) + part
        highest, scores = new, later
    sums = total[:, HDIM:]
    out_ref[0, :rows] = (total[:, :HDIM] / sums).astype(jnp.bfloat16)
    logs = highest * SCALE + jnp.log(sums) * LOG2E
    same, line = diagonal(), lax.broadcasted_iota(jnp.int32, (8, HDIM), 0)
    packed = jnp.zeros((8, HDIM), jnp.float32)
    for b in range(rows // HDIM):
        part = logs[b * HDIM : (b + 1) * HDIM]
        row = jnp.sum(jnp.where(same, part, 0.0), axis=0, keepdims=True)
        packed = jnp.where(line == b, row, packed)
    high = packed.astype(jnp.bfloat16).astype(jnp.float32)
    middle = (packed - high).astype(jnp.bfloat16).astype(jnp.float32)
    low = packed - high - middle
    out_ref[0, rows:] = jnp.concatenate(
        [high, middle, low, jnp.zeros_like(low)], axis=0
    ).astype(jnp.bfloat16)


def attend(queries, pairs):
    groups, heads, each, _ = queries.shape
    rows = groups * each
    pair = lambda a: pl.BlockSpec((a.shape[0], 2, each, HDIM), lambda h: (0, h, 0, 0))
    keys = sum(a.shape[0] for a in pairs) * each
    scores = heads * rows * keys
    return pl.pallas_call(
        attend_kernel,
        grid=(heads,),
        in_specs=[pl.BlockSpec((groups, 1, each, HDIM), lambda h: (0, h, 0, 0))]
        + [pair(a) for a in pairs],
        out_specs=pl.BlockSpec((1, rows + EXTRA, HDIM), lambda h: (h, 0, 0)),
        out_shape=jax.ShapeDtypeStruct((heads, rows + EXTRA, HDIM), jnp.bfloat16),
        compiler_params=params(48),
        cost_estimate=pl.CostEstimate(
            flops=scores * HDIM * 4 * 4,
            bytes_accessed=heads * keys * HDIM * 4,
            transcendentals=scores,
        ),
    )(queries, *pairs)


def merge_kernel(a_ref, b_ref, out_ref):
    groups, heads, rows, _ = out_ref.shape
    tokens = groups * rows
    same = diagonal()

    def logs(ref, h):
        extra = ref[h, tokens:].astype(jnp.float32)
        return extra[0:8] + extra[8:16] + extra[16:24]

    for h in range(heads):
        difference = logs(b_ref, h) - logs(a_ref, h)
        share = 1.0 / (1.0 + jnp.exp2(difference))
        columns = [
            jnp.sum(jnp.where(same, share[r : r + 1], 0.0), axis=1, keepdims=True)
            for r in range(tokens // HDIM)
        ]
        column = jnp.concatenate(columns, axis=0)
        for g in range(groups):
            part = slice(g * rows, (g + 1) * rows)
            a, b = a_ref[h, part].astype(jnp.float32), b_ref[h, part].astype(jnp.float32)
            out_ref[g, h] = (b + (a - b) * column[part]).astype(jnp.bfloat16)


def merge(a, b, groups):
    heads, tokens = a.shape[0], a.shape[1] - EXTRA
    shape = (groups, heads, tokens // groups, HDIM)
    return pl.pallas_call(
        merge_kernel,
        out_shape=jax.ShapeDtypeStruct(shape, jnp.bfloat16),
        compiler_params=params(16),
    )(a, b)


def project_kernel(c_ref, *refs, pieces):
    low_refs, high_refs = refs[:pieces], refs[pieces : 2 * pieces]
    near_ref, far_ref, *out_refs, near, far = refs[2 * pieces :]
    step, steps = pl.program_id(0), pl.num_programs(0)
    groups, heads, rows, _ = low_refs[0].shape
    flat = lambda ref: jnp.concatenate([ref[g, h] for g in range(groups) for h in range(heads)], axis=1)
    attention = jnp.concatenate(
        [jnp.where(step < steps // 2, flat(low), flat(high)) for low, high in zip(low_refs, high_refs)],
        axis=0,
    )
    for weight_ref, total in ((near_ref, near), (far_ref, far)):
        part = jnp.dot(attention, weight_ref[...], preferred_element_type=jnp.float32)

        @pl.when(step == 0)
        def _(part=part, total=total):
            total[...] = part

        @pl.when(step > 0)
        def _(part=part, total=total):
            total[...] += part

    @pl.when(step == steps - 1)
    def _():
        columns = near.shape[1]
        for total, at in ((near, c_ref[0]), (far, 1 - c_ref[0])):
            place = pl.ds(pl.multiple_of(at * columns, HDIM), columns)
            for p, out_ref in enumerate(out_refs):
                out_ref[:, place] = total[p * rows : (p + 1) * rows].astype(out_ref.dtype)


def project(c, pieces, near, far):
    depth, columns = near.shape
    steps = 4
    lows, highs = [piece[0] for piece in pieces], [piece[-1] for piece in pieces]
    _, heads, rows, _ = lows[0].shape
    groups = depth // heads // HDIM // steps
    part = (groups, heads, rows, HDIM)
    low = pl.BlockSpec(part, lambda i, c: (jnp.minimum(i, steps // 2 - 1), 0, 0, 0))

    def high(piece):
        first = 0 if len(piece) == 2 else steps // 2
        return pl.BlockSpec(part, lambda i, c: (jnp.maximum(i - steps // 2, 0) + first, 0, 0, 0))

    weight = pl.BlockSpec((depth // steps, columns), lambda i, c: (i, 0))
    out = jax.ShapeDtypeStruct((rows, 2 * columns), jnp.bfloat16)
    return pl.pallas_call(
        functools.partial(project_kernel, pieces=len(pieces)),
        grid_spec=pltpu.PrefetchScalarGridSpec(
            num_scalar_prefetch=1,
            grid=(steps,),
            in_specs=[low] * len(pieces) + [high(piece) for piece in pieces] + [weight, weight],
            out_specs=[pl.BlockSpec(out.shape, lambda i, c: (0, 0))] * len(pieces),
            scratch_shapes=[pltpu.VMEM((len(pieces) * rows, columns), jnp.float32)] * 2,
        ),
        out_shape=[out] * len(pieces),
        compiler_params=params(16),
    )(c, *lows, *highs, near, far)


def place_kernel(x_ref, *refs):
    *in_refs, out_ref = refs
    columns = in_refs[0].shape[1]
    for i, ref in enumerate(in_refs):
        at = lax.rem(x_ref[0] + i, len(in_refs)) * columns
        out_ref[:, pl.ds(pl.multiple_of(at, HDIM), columns)] = ref[...]


def place(x, pieces):
    rows, columns = pieces[0].shape
    whole = pl.BlockSpec((rows, columns), lambda i, x: (0, 0))
    return pl.pallas_call(
        place_kernel,
        grid_spec=pltpu.PrefetchScalarGridSpec(
            num_scalar_prefetch=1,
            grid=(1,),
            in_specs=[whole] * len(pieces),
            out_specs=pl.BlockSpec((rows, len(pieces) * columns), lambda i, x: (0, 0)),
        ),
        out_shape=jax.ShapeDtypeStruct((rows, len(pieces) * columns), pieces[0].dtype),
        compiler_params=params(16),
    )(x, *pieces)


def per_device(queries, keys, values, out_weight):
    groups, across = lax.axis_size("z"), lax.axis_size("x")
    x, c = (lax.axis_index(axis).astype(jnp.int32)[None] for axis in ("x", "c"))
    half = out_weight.shape[1] // across // 2

    grouped, pairs, columns = regroup(2 * x + c, queries, keys, values, out_weight, half, groups)
    pairs = lax.all_to_all(pairs, "z", 0, 0, tiled=True)
    weight = lax.all_gather(after(columns, pairs), "z", axis=0, tiled=True)
    own, behind, ahead, over = two_steps(pairs, "x")
    q = lax.all_to_all(after(grouped, pairs), "z", 0, 0, tiled=True)
    q_beside = shift(after(q, *behind, *ahead), "y", 1)

    every = [part for p in (own, behind, ahead, over) for part in (*p, *(shift(b, "c", 1) for b in p))]
    partial_beside = attend(q_beside, every)
    partial = attend(after(q, partial_beside), every)
    attention = merge(partial, shift(partial_beside, "y", 1), groups)
    weight_beside = shift(after(weight, attention), "c", 1)

    back = lax.all_to_all(attention, "z", 0, 0, tiled=True)
    own, behind, ahead, over = ring(back, "x")
    returned, done = [], ()
    for pieces, distances in (((own, behind, ahead), (0, 1, -1)), ((over,), (2,))):
        pieces = [[after(part, *done) for part in piece] for piece in pieces]
        done = project(c, pieces, weight, weight_beside)
        returned += [shift(block, "x", -distance) for block, distance in zip(done, distances)]
    own, ahead, behind, over = returned
    return place(x, [own, ahead, over, behind])


def solution(mesh):
    clip, blk, z = mesh.devices.shape
    devices = np.array(mesh.devices).reshape(clip, blk // 4, 2, 2, z)
    tokens = ("clip", "x", "y", "c", "z")
    return jax.shard_map(
        per_device,
        mesh=Mesh(devices, tokens),
        in_specs=(P(tokens, None), P(tokens, None), P(tokens, None), P("z", None)),
        out_specs=P(tokens, None),
        check_vma=False,
    )
```

```python
import functools

import jax
import jax.numpy as jnp
import numpy as np
from jax import lax
from jax.experimental import pallas as pl
from jax.experimental.pallas import tpu as pltpu
from jax.sharding import Mesh
from jax.sharding import PartitionSpec as P

HDIM = 128
LOG2E = 1.4426950408889634
SCALE = HDIM**-0.5 * LOG2E
EXTRA = 32


def shift(block, axis, distance):
    n = lax.axis_size(axis)
    if distance % n == 0:
        return block
    return lax.ppermute(block, axis, [(i, (i + distance) % n) for i in range(n)])


def ring(block, axis):
    middle = block.shape[0] // 2
    low, high = block[:middle], block[middle:]
    behind_low, ahead_high = shift(low, axis, 1), shift(high, axis, -1)
    behind_high, ahead_low = shift(high, axis, 1), shift(low, axis, -1)
    across = [shift(behind_low, axis, 1), shift(ahead_high, axis, -1)]
    return [block], [behind_low, behind_high], [ahead_low, ahead_high], across


def two_steps(block, axis):
    behind, ahead = shift(block, axis, 1), shift(block, axis, -1)
    middle = block.shape[0] // 2
    return [block], [behind], [ahead], [shift(behind[:middle], axis, 1), shift(ahead[middle:], axis, -1)]


def after(value, *done):
    return lax.optimization_barrier((value, *done))[0]


def params(mebibytes):
    return pltpu.CompilerParams(vmem_limit_bytes=mebibytes * 1024 * 1024)


def regroup_kernel(at_ref, q_ref, k_ref, v_ref, weight_ref, queries_ref, pairs_ref, columns_ref):
    groups, heads = queries_ref.shape[:2]
    for g in range(groups):
        for h in range(heads):
            part = slice((g * heads + h) * HDIM, (g * heads + h + 1) * HDIM)
            queries_ref[g, h] = q_ref[:, part]
            pairs_ref[g, 2 * h] = k_ref[:, part]
            pairs_ref[g, 2 * h + 1] = v_ref[:, part]
    columns_ref[...] = weight_ref[...]


def regroup(at, queries, keys, values, out_weight, columns, groups):
    rows, full = queries.shape
    heads = full // groups // HDIM
    block = pl.BlockSpec((out_weight.shape[0], columns), lambda i, at: (0, at[0]))
    whole = lambda a: pl.BlockSpec(a.shape, lambda i, at: (0,) * len(a.shape))
    shapes = [
        jax.ShapeDtypeStruct((groups, heads, rows, HDIM), queries.dtype),
        jax.ShapeDtypeStruct((groups, 2 * heads, rows, HDIM), queries.dtype),
        jax.ShapeDtypeStruct((out_weight.shape[0], columns), out_weight.dtype),
    ]
    return pl.pallas_call(
        regroup_kernel,
        grid_spec=pltpu.PrefetchScalarGridSpec(
            num_scalar_prefetch=1,
            grid=(1,),
            in_specs=[whole(queries)] * 3 + [block],
            out_specs=[whole(a) for a in shapes],
        ),
        out_shape=shapes,
        compiler_params=params(56),
    )(at, queries, keys, values, out_weight)


def diagonal():
    shape = (HDIM, HDIM)
    return lax.broadcasted_iota(jnp.int32, shape, 0) == lax.broadcasted_iota(jnp.int32, shape, 1)


def attend_kernel(q_ref, *refs):
    *pair_refs, out_ref = refs
    groups, _, each, _ = q_ref.shape
    rows = groups * each
    q = q_ref[:, 0].reshape(rows, HDIM)
    tiles, held = [[]], 0
    for ref in pair_refs:
        if held == 2 * groups:
            tiles, held = tiles + [[]], 0
        tiles[-1].append(ref)
        held += ref.shape[0]

    def tile(i, which):
        parts = [ref[:, which].reshape(-1, HDIM) for ref in tiles[i]]
        return jnp.concatenate(parts, axis=0)

    def scores_of(i):
        return lax.dot_general(
            q, tile(i, 0), (((1,), (1,)), ((), ())), preferred_element_type=jnp.float32
        )

    highest, total = None, None
    scores = scores_of(0)
    for i in range(len(tiles)):
        later = scores_of(i + 1) if i + 1 < len(tiles) else None
        value = tile(i, 1)
        value = jnp.concatenate([value, jnp.ones_like(value)], axis=1)
        tile_max = jnp.max(scores, axis=1, keepdims=True)
        new = tile_max if highest is None else jnp.maximum(highest, tile_max)
        weights = jnp.exp2((scores - new) * SCALE).astype(jnp.bfloat16)
        part = jnp.dot(weights, value, preferred_element_type=jnp.float32)
        if highest is None:
            total = part
        else:
            total = total * jnp.exp2((highest - new) * SCALE) + part
        highest, scores = new, later
    sums = total[:, HDIM:]
    out_ref[0, :rows] = (total[:, :HDIM] / sums).astype(jnp.bfloat16)
    logs = highest * SCALE + jnp.log(sums) * LOG2E
    same, line = diagonal(), lax.broadcasted_iota(jnp.int32, (8, HDIM), 0)
    packed = jnp.zeros((8, HDIM), jnp.float32)
    for b in range(rows // HDIM):
        part = logs[b * HDIM : (b + 1) * HDIM]
        row = jnp.sum(jnp.where(same, part, 0.0), axis=0, keepdims=True)
        packed = jnp.where(line == b, row, packed)
    high = packed.astype(jnp.bfloat16).astype(jnp.float32)
    middle = (packed - high).astype(jnp.bfloat16).astype(jnp.float32)
    low = packed - high - middle
    out_ref[0, rows:] = jnp.concatenate(
        [high, middle, low, jnp.zeros_like(low)], axis=0
    ).astype(jnp.bfloat16)


def attend(queries, pairs):
    groups, heads, each, _ = queries.shape
    rows = groups * each
    pair = lambda a: pl.BlockSpec((a.shape[0], 2, each, HDIM), lambda h: (0, h, 0, 0))
    keys = sum(a.shape[0] for a in pairs) * each
    scores = heads * rows * keys
    return pl.pallas_call(
        attend_kernel,
        grid=(heads,),
        in_specs=[pl.BlockSpec((groups, 1, each, HDIM), lambda h: (0, h, 0, 0))]
        + [pair(a) for a in pairs],
        out_specs=pl.BlockSpec((1, rows + EXTRA, HDIM), lambda h: (h, 0, 0)),
        out_shape=jax.ShapeDtypeStruct((heads, rows + EXTRA, HDIM), jnp.bfloat16),
        compiler_params=params(48),
        cost_estimate=pl.CostEstimate(
            flops=scores * HDIM * 4 * 4,
            bytes_accessed=heads * keys * HDIM * 4,
            transcendentals=scores,
        ),
    )(queries, *pairs)


def merge_kernel(a_ref, b_ref, out_ref):
    groups, heads, rows, _ = out_ref.shape
    tokens = groups * rows
    same = diagonal()

    def logs(ref, h):
        extra = ref[h, tokens:].astype(jnp.float32)
        return extra[0:8] + extra[8:16] + extra[16:24]

    for h in range(heads):
        difference = logs(b_ref, h) - logs(a_ref, h)
        share = 1.0 / (1.0 + jnp.exp2(difference))
        columns = [
            jnp.sum(jnp.where(same, share[r : r + 1], 0.0), axis=1, keepdims=True)
            for r in range(tokens // HDIM)
        ]
        column = jnp.concatenate(columns, axis=0)
        for g in range(groups):
            part = slice(g * rows, (g + 1) * rows)
            a, b = a_ref[h, part].astype(jnp.float32), b_ref[h, part].astype(jnp.float32)
            out_ref[g, h] = (b + (a - b) * column[part]).astype(jnp.bfloat16)


def merge(a, b, groups):
    heads, tokens = a.shape[0], a.shape[1] - EXTRA
    shape = (groups, heads, tokens // groups, HDIM)
    return pl.pallas_call(
        merge_kernel,
        out_shape=jax.ShapeDtypeStruct(shape, jnp.bfloat16),
        compiler_params=params(16),
    )(a, b)


def project_kernel(c_ref, *refs, pieces):
    low_refs, high_refs = refs[:pieces], refs[pieces : 2 * pieces]
    near_ref, far_ref, *out_refs, near, far = refs[2 * pieces :]
    step, steps = pl.program_id(0), pl.num_programs(0)
    groups, heads, rows, _ = low_refs[0].shape
    flat = lambda ref: jnp.concatenate([ref[g, h] for g in range(groups) for h in range(heads)], axis=1)
    attention = jnp.concatenate(
        [jnp.where(step < steps // 2, flat(low), flat(high)) for low, high in zip(low_refs, high_refs)],
        axis=0,
    )
    for weight_ref, total in ((near_ref, near), (far_ref, far)):
        part = jnp.dot(attention, weight_ref[...], preferred_element_type=jnp.float32)

        @pl.when(step == 0)
        def _(part=part, total=total):
            total[...] = part

        @pl.when(step > 0)
        def _(part=part, total=total):
            total[...] += part

    @pl.when(step == steps - 1)
    def _():
        columns = near.shape[1]
        for total, at in ((near, c_ref[0]), (far, 1 - c_ref[0])):
            place = pl.ds(pl.multiple_of(at * columns, HDIM), columns)
            for p, out_ref in enumerate(out_refs):
                out_ref[:, place] = total[p * rows : (p + 1) * rows].astype(out_ref.dtype)


def project(c, pieces, near, far):
    depth, columns = near.shape
    steps = 4
    lows, highs = [piece[0] for piece in pieces], [piece[-1] for piece in pieces]
    _, heads, rows, _ = lows[0].shape
    groups = depth // heads // HDIM // steps
    part = (groups, heads, rows, HDIM)
    low = pl.BlockSpec(part, lambda i, c: (jnp.minimum(i, steps // 2 - 1), 0, 0, 0))

    def high(piece):
        first = 0 if len(piece) == 2 else steps // 2
        return pl.BlockSpec(part, lambda i, c: (jnp.maximum(i - steps // 2, 0) + first, 0, 0, 0))

    weight = pl.BlockSpec((depth // steps, columns), lambda i, c: (i, 0))
    out = jax.ShapeDtypeStruct((rows, 2 * columns), jnp.bfloat16)
    return pl.pallas_call(
        functools.partial(project_kernel, pieces=len(pieces)),
        grid_spec=pltpu.PrefetchScalarGridSpec(
            num_scalar_prefetch=1,
            grid=(steps,),
            in_specs=[low] * len(pieces) + [high(piece) for piece in pieces] + [weight, weight],
            out_specs=[pl.BlockSpec(out.shape, lambda i, c: (0, 0))] * len(pieces),
            scratch_shapes=[pltpu.VMEM((len(pieces) * rows, columns), jnp.float32)] * 2,
        ),
        out_shape=[out] * len(pieces),
        compiler_params=params(56),
    )(c, *lows, *highs, near, far)


def place_kernel(x_ref, *refs):
    *in_refs, out_ref = refs
    columns = in_refs[0].shape[1]
    for i, ref in enumerate(in_refs):
        at = lax.rem(x_ref[0] + i, len(in_refs)) * columns
        out_ref[:, pl.ds(pl.multiple_of(at, HDIM), columns)] = ref[...]


def place(x, pieces):
    rows, columns = pieces[0].shape
    whole = pl.BlockSpec((rows, columns), lambda i, x: (0, 0))
    return pl.pallas_call(
        place_kernel,
        grid_spec=pltpu.PrefetchScalarGridSpec(
            num_scalar_prefetch=1,
            grid=(1,),
            in_specs=[whole] * len(pieces),
            out_specs=pl.BlockSpec((rows, len(pieces) * columns), lambda i, x: (0, 0)),
        ),
        out_shape=jax.ShapeDtypeStruct((rows, len(pieces) * columns), pieces[0].dtype),
        compiler_params=params(16),
    )(x, *pieces)


def per_device(queries, keys, values, out_weight):
    groups, across = lax.axis_size("z"), lax.axis_size("x")
    x, c = (lax.axis_index(axis).astype(jnp.int32)[None] for axis in ("x", "c"))
    half = out_weight.shape[1] // across // 2

    grouped, pairs, columns = regroup(2 * x + c, queries, keys, values, out_weight, half, groups)
    pairs = lax.all_to_all(pairs, "z", 0, 0, tiled=True)
    weight = lax.all_gather(after(columns, pairs), "z", axis=0, tiled=True)
    own, behind, ahead, over = two_steps(pairs, "x")
    q = lax.all_to_all(after(grouped, pairs), "z", 0, 0, tiled=True)
    q_beside = shift(after(q, *behind, *ahead), "y", 1)

    every = [part for p in (own, behind, ahead, over) for part in (*p, *(shift(b, "c", 1) for b in p))]
    partial_beside = attend(q_beside, every)
    partial = attend(after(q, partial_beside), every)
    attention = merge(partial, shift(partial_beside, "y", 1), groups)
    weight_beside = shift(after(weight, attention), "c", 1)

    back = lax.all_to_all(attention, "z", 0, 0, tiled=True)
    own, behind, ahead, over = ring(back, "x")
    returned, done = [], ()
    for pieces, distances in (((own, behind, ahead), (0, 1, -1)), ((over,), (2,))):
        pieces = [[after(part, *done) for part in piece] for piece in pieces]
        done = project(c, pieces, weight, weight_beside)
        returned += [shift(block, "x", -distance) for block, distance in zip(done, distances)]
    own, ahead, behind, over = returned
    return place(x, [own, ahead, over, behind])


def solution(mesh):
    clip, blk, z = mesh.devices.shape
    devices = np.array(mesh.devices).reshape(clip, blk // 4, 2, 2, z)
    tokens = ("clip", "x", "y", "c", "z")
    return jax.shard_map(
        per_device,
        mesh=Mesh(devices, tokens),
        in_specs=(P(tokens, None), P(tokens, None), P(tokens, None), P("z", None)),
        out_specs=P(tokens, None),
        check_vma=False,
    )
```
